32 devices in a mesh: front: 4 (over z), helper: 8 (over y, x, core).
Axes of the slice: x: 2, y: 2, z: 4, core: 2. Of those that a mesh axis runs over, the one named last changes fastest.
Arguments:
- front: float32 [4, 4096, 4096], P('front', 'helper')
- row_list: int32 [4, 4096], replicated, may hold values from 0 to 4095, as said below
- child_map: int32 [4, 3840], replicated, may hold values from 0 to 8191, as said below
- parent: float32 [8192, 8192], P(('front', 'helper')), may hold values from -6 to 6
Outputs:
- factors: float32 [4, 4096, 4096], P('front', 'helper')
- assembled: float32 [8192, 8192], P(('front', 'helper'))
The draws below stay inside these ranges and needn't reach their ends.
Inputs may be any that keep to these rules, and one draw needn't show every extreme that they name: Each row of row_list is a permutation; stored rows h * 512 to (h + 1) * 512 - 1 of a front lie on helper h. Of the 256 rows of any panel, one helper holds at most 48, and some helper holds exactly 48 in every panel. The leading 256 x 256 block of every front is well conditioned without pivoting: its diagonal exceeds 2.5 sqrt(256) times the row's spread. `child_map`: distinct within a front. Parent row r lies on device r // 256 of front+helper. Of the contribution rows on one device, at most 16 go to one device's parent rows, and exactly 16 go to some device.
All inputs are finite; a program needn't handle non-finite values.
Results may differ from the reference program's by a relative error of at most 0.0001.
Values sent between devices are 32-bit elements; how exact they have to be, the bound alone decides.
A program may use at most 128 MiB of HBM per device.

```python
import jax
import jax.numpy as jnp
from jax import lax

FRONT_ORDER = 4096
PANEL = 256
PANELS = 1
PARENT_ORDER = 8192
FRONTS = 4
ROWS_DEV = 512
PIVOTS = 256
CB_ORDER = 3840
XCAP = 16
PARENT_ROWS = 256


def one_front(front_key, base_counts):
    helpers = FRONT_ORDER // ROWS_DEV
    devices_all = FRONTS * helpers
    blocks_each = (ROWS_DEV + XCAP - 1) // XCAP
    key_list = jax.random.split(front_key, 6)
    helper_perms = jax.vmap(lambda sub: jax.random.permutation(sub, helpers))(jax.random.split(key_list[0], PANELS))
    counts = base_counts[helper_perms].T
    bounds = jnp.concatenate([jnp.zeros((helpers, 1), jnp.int32), jnp.cumsum(counts, axis=1)], axis=1)
    slot_iota = jnp.arange(ROWS_DEV, dtype=jnp.int32)
    labels = jnp.sum((slot_iota[None, :, None] >= bounds[:, None, 1:]).astype(jnp.int32), axis=2)
    within = slot_iota[None, :] - jnp.take_along_axis(bounds, labels, axis=1)
    offsets = jnp.cumsum(counts, axis=0) - counts
    safe_labels = jnp.minimum(labels, PANELS - 1)
    panel_slot = jnp.take_along_axis(offsets, safe_labels, axis=1) + within
    panel_perms = jax.vmap(lambda sub: jax.random.permutation(sub, PANEL))(jax.random.split(key_list[1], PANELS))
    panel_rows = safe_labels * PANEL + panel_perms[safe_labels, jnp.clip(panel_slot, 0, PANEL - 1)]
    cb_count = ROWS_DEV - bounds[:, PANELS]
    cb_offsets = jnp.cumsum(cb_count) - cb_count
    cb_perm = jax.random.permutation(key_list[2], CB_ORDER)
    cb_slot = jnp.clip(cb_offsets[:, None] + within, 0, CB_ORDER - 1)
    cb_rows = PIVOTS + cb_perm[cb_slot]
    is_cb = labels == PANELS
    row_ids = jnp.where(is_cb, cb_rows, panel_rows)
    owner_perm = jax.random.permutation(key_list[3], devices_all)
    block_index = jnp.clip(within // XCAP, 0, blocks_each - 1)
    pick_index = jnp.arange(helpers, dtype=jnp.int32)[:, None] * blocks_each + block_index
    owners = owner_perm[pick_index % devices_all]
    arrival = pick_index // devices_all * XCAP + within % XCAP
    slot_perms = jax.vmap(lambda sub: jax.random.permutation(sub, PARENT_ROWS))(jax.random.split(key_list[4], devices_all))
    targets = owners * PARENT_ROWS + slot_perms[owners, jnp.clip(arrival, 0, PARENT_ROWS - 1)]
    place = jnp.where(is_cb, row_ids - PIVOTS, CB_ORDER).reshape(-1)
    parent_map = jnp.zeros((CB_ORDER,), jnp.int32).at[place].set(targets.reshape(-1).astype(jnp.int32), mode='drop')
    shuffle = jax.vmap(lambda sub: jax.random.permutation(sub, ROWS_DEV))(jax.random.split(key_list[5], helpers))
    stored = jnp.take_along_axis(row_ids, shuffle, axis=1).reshape(FRONT_ORDER)
    return (stored.astype(jnp.int32), parent_map)


def layout(key):
    helpers = FRONT_ORDER // ROWS_DEV
    per_helper = PANEL // helpers
    half_count = helpers // 2
    helper_iota = jnp.arange(helpers, dtype=jnp.int32)
    mirror = jnp.minimum(helper_iota, helpers - 1 - helper_iota)
    swing = per_helper // 2 * (half_count - mirror) // max(half_count, 1)
    base_counts = jnp.where(helper_iota < half_count, per_helper + swing, per_helper - swing).astype(jnp.int32)
    front_keys = jax.random.split(key, FRONTS)
    return jax.vmap(lambda sub: one_front(sub, base_counts))(front_keys)


def draw_row_list(key, part):
    stored, parent_map = layout(key)
    return stored


def draw_child_map(key, part):
    stored, parent_map = layout(key)
    return parent_map


def draw_front(key, part):
    stored, parent_map = layout(key)
    key = jax.random.fold_in(key, 3)
    value_key, diag_key = jax.random.split(key, 2)
    shape = (FRONTS, FRONT_ORDER, FRONT_ORDER)
    values = jnp.clip(jax.random.normal(value_key, shape, jnp.float32), -6.0, 6.0)
    diagonal = PIVOTS ** 0.5 * jax.random.uniform(diag_key, (FRONTS, FRONT_ORDER, 1), jnp.float32, 2.5, 4.0)
    columns = jnp.arange(FRONT_ORDER, dtype=jnp.int32)
    full = jnp.where(columns[None, None, :] == stored[:, :, None], diagonal, values)
    return full.astype(jnp.float32)


def shard_levels(rng, dims, cuts, least, high):
    gain = 1.0
    for position, parts in cuts:
        heights = jax.random.uniform(jax.random.fold_in(jax.random.fold_in(rng, 6), position), (parts,), jnp.float32, least / len(cuts), high / len(cuts))
        gain = gain * jnp.repeat(jnp.exp(heights), dims[position] // parts).reshape((-1,) + (1,) * (len(dims) - 1 - position))
    return gain


def bell_draw(own_key, shape, deviation, limit, shards=(), kind=jnp.bfloat16):
    array = deviation * jax.random.normal(own_key, shape, jnp.float32)
    if shards:
        array = array * shard_levels(own_key, shape, shards, -0.22, 0.18)
    return jnp.clip(array, -limit, limit).astype(kind)


def setup_inputs(seed: int = 0) -> dict:
    keys = jax.random.split(jax.random.key(seed), 5)
    return {
        "front": draw_front(jax.random.fold_in(keys[4], 71), 0),
        "row_list": draw_row_list(jax.random.fold_in(keys[4], 71), 0),
        "child_map": draw_child_map(jax.random.fold_in(keys[4], 71), 0),
        "parent": bell_draw(keys[3], (PARENT_ORDER, PARENT_ORDER), 1.0, 6.0, ((0, 32),), jnp.float32),
    }


def product(left, right):
    return jnp.dot(left, right, precision=lax.Precision.HIGHEST, preferred_element_type=jnp.float32)


def small_inverse(matrix):
    extent = matrix.shape[0]
    augmented = jnp.concatenate([matrix, jnp.eye(extent, dtype=matrix.dtype)], axis=1)
    for column in range(extent):
        pivot_row = augmented[column] / augmented[column, column]
        augmented = augmented - augmented[:, column:column + 1] * pivot_row[None, :]
        augmented = augmented.at[column].set(pivot_row)
    return augmented[:, extent:]


def block_inverse(matrix):
    extent = matrix.shape[0]
    if extent <= 32:
        return small_inverse(matrix)
    middle = extent // 2
    upper_left = matrix[:middle, :middle]
    upper_right = matrix[:middle, middle:]
    lower_left = matrix[middle:, :middle]
    lower_right = matrix[middle:, middle:]
    inverse_left = block_inverse(upper_left)
    coupled = product(inverse_left, upper_right)
    schur_part = lower_right - product(lower_left, coupled)
    inverse_schur = block_inverse(schur_part)
    left_factor = product(lower_left, inverse_left)
    top_right = -product(coupled, inverse_schur)
    bottom_left = -product(inverse_schur, left_factor)
    top_left = inverse_left - product(top_right, left_factor)
    upper_half = jnp.concatenate([top_left, top_right], axis=1)
    lower_half = jnp.concatenate([bottom_left, inverse_schur], axis=1)
    return jnp.concatenate([upper_half, lower_half], axis=0)


def eliminate(stored, row_order):
    natural = jnp.zeros_like(stored).at[row_order].set(stored)
    for panel_index in range(PANELS):
        first_col = panel_index * PANEL
        end_col = first_col + PANEL
        inverse = block_inverse(natural[first_col:end_col, first_col:end_col])
        lower_part = product(natural[end_col:, first_col:end_col], inverse)
        natural = natural.at[end_col:, first_col:end_col].set(lower_part)
        natural = natural.at[end_col:, end_col:].add(-product(lower_part, natural[first_col:end_col, end_col:]))
    return natural[row_order], natural[PIVOTS:, PIVOTS:]


def reference(front, row_list, child_map, parent):
    assembled = parent
    factor_list = []
    for front_index in range(FRONTS):
        done, contribution = eliminate(front[front_index], row_list[front_index])
        factor_list.append(done)
        targets = child_map[front_index]
        assembled = assembled.at[targets[:, None], targets[None, :]].add(contribution)
    return jnp.stack(factor_list), assembled
```

```python
import jax
import jax.numpy as jnp
from jax import lax
from jax.experimental import pallas as pl
from jax.experimental.pallas import tpu as pltpu
from jax.sharding import PartitionSpec as P

PANEL = 256
PIVOTS = 256
LANES = 128
BLOCK = 32
CHUNKS = 2


def product(left, right, precision=lax.Precision.HIGHEST):
    return jnp.dot(left, right, precision=precision, preferred_element_type=jnp.float32)


def inverse_kernel(matrix_ref, out_ref):
    extent = matrix_ref.shape[0]
    out_ref[...] = matrix_ref[...]
    row_iota = lax.broadcasted_iota(jnp.int32, (BLOCK, 1), 0)
    lane_iota = lax.broadcasted_iota(jnp.int32, (1, extent), 1)
    for start in range(0, extent, BLOCK):
        rows = out_ref[start : start + BLOCK, :]
        for step in range(BLOCK):
            lane = start + step
            column = rows[:, lane : lane + 1]
            pivot_row = rows[step : step + 1, :]
            scale = 1.0 / column[step : step + 1, :]
            at_lane = lane_iota == lane
            scaled = jnp.where(at_lane, scale, pivot_row * scale)
            weight = jnp.where(row_iota == step, -1.0, column)
            keep = jnp.where(at_lane | (row_iota == step), 0.0, rows)
            rows = keep - weight * scaled
        out_ref[start : start + BLOCK, :] = rows
        tile = start // LANES * LANES
        tile_lane = tile + lax.broadcasted_iota(jnp.int32, (1, LANES), 1)
        all_row = lax.broadcasted_iota(jnp.int32, (extent, 1), 0)
        outside = (all_row < start) | (all_row >= start + BLOCK)
        inside_lane = (tile_lane >= start) & (tile_lane < start + BLOCK)
        left = jnp.where(outside & inside_lane, out_ref[:, tile : tile + LANES], 0.0)
        update = product(left, out_ref[tile : tile + LANES, :])
        cleared = outside & (lane_iota >= start) & (lane_iota < start + BLOCK)
        out_ref[...] = jnp.where(cleared, 0.0, out_ref[...]) - update


def block_inverse(matrix):
    extent = matrix.shape[0]
    return pl.pallas_call(
        inverse_kernel,
        out_shape=jax.ShapeDtypeStruct((extent, extent), jnp.float32),
        in_specs=[pl.BlockSpec(memory_space=pltpu.VMEM)],
        out_specs=pl.BlockSpec(memory_space=pltpu.VMEM),
        compiler_params=pltpu.CompilerParams(vmem_limit_bytes=16 * 1024 * 1024),
        cost_estimate=pl.CostEstimate(flops=10**9, bytes_accessed=10**8, transcendentals=0),
        name="panel_inverse",
    )(matrix)


def spread_kernel(map_ref, target_ref, received_ref, base_ref, out_ref, turned, spread):
    front = pl.program_id(0)
    width = received_ref.shape[2]
    slots = received_ref.shape[1]
    parent_rows, parent_width = out_ref.shape

    @pl.when(front == 0)
    def _():
        out_ref[...] = base_ref[...]

    spread[...] = jnp.zeros_like(spread)
    for first in range(0, width, LANES):
        turned[first : first + LANES, :] = received_ref[0, :, first : first + LANES].T

    @pl.loop(0, width // 16)
    def _(group):
        base = group * 16
        for offset in range(16):
            place = map_ref[front, base + offset]
            spread[pl.ds(place, 1), :] = turned[pl.ds(base + offset, 1), :]

    row_iota = lax.broadcasted_iota(jnp.int32, (parent_rows, slots), 0)
    pick = (row_iota == target_ref[0].astype(jnp.int32)).astype(jnp.bfloat16)
    pick = jnp.concatenate([pick, pick], axis=1)
    piece = 512

    @pl.loop(0, parent_width // piece)
    def _(index):
        at = pl.ds(pl.multiple_of(index * piece, piece), piece)
        block = spread[at, :]
        high = block.astype(jnp.bfloat16)
        low = (block - high.astype(jnp.float32)).astype(jnp.bfloat16)
        both = jnp.concatenate([high, low], axis=1)
        out_ref[:, at] += lax.dot_general(
            pick, both, (((1,), (1,)), ((), ())), preferred_element_type=jnp.float32
        )


def spread_add(columns, targets, received, base):
    fronts, slots, width = received.shape
    parent_rows, parent_width = base.shape
    return pl.pallas_call(
        spread_kernel,
        grid=(fronts,),
        out_shape=jax.ShapeDtypeStruct(base.shape, jnp.float32),
        in_specs=[
            pl.BlockSpec(memory_space=pltpu.SMEM),
            pl.BlockSpec((1, 1, slots), lambda front: (front, 0, 0)),
            pl.BlockSpec((1, slots, width), lambda front: (front, 0, 0)),
            pl.BlockSpec((parent_rows, parent_width), lambda front: (0, 0), pipeline_mode=pl.Buffered(1)),
        ],
        out_specs=pl.BlockSpec((parent_rows, parent_width), lambda front: (0, 0)),
        scratch_shapes=[
            pltpu.VMEM((width, slots), jnp.float32),
            pltpu.VMEM((parent_width, slots), jnp.float32),
        ],
        compiler_params=pltpu.CompilerParams(vmem_limit_bytes=48 * 1024 * 1024),
        cost_estimate=pl.CostEstimate(
            flops=4 * fronts * parent_rows * slots * parent_width,
            bytes_accessed=100 * 10**6,
            transcendentals=0,
        ),
        name="spread_add",
    )(columns, targets, received, base)


def local(front, row_list, child_map, parent):
    front_rows = front[0]
    row_count = front_rows.shape[0]
    helpers = lax.axis_size("helper")
    fronts = lax.axis_size("front")
    devices_all = helpers * fronts
    my_front = lax.axis_index("front")
    my_helper = lax.axis_index("helper")
    parent_rows = parent.shape[0]
    cb_width = front_rows.shape[1] - PIVOTS
    cap_rows = (row_count + devices_all - 1) // devices_all
    cap_panel = 3 * PANEL // (2 * helpers)
    front_order = jnp.take(row_list, my_front, axis=0)
    own_ids = lax.dynamic_slice_in_dim(front_order, my_helper * row_count, row_count)

    by_helper = front_order.reshape(helpers, row_count)
    in_panel = by_helper < PANEL
    panel_rank = jnp.cumsum(in_panel.astype(jnp.int32), axis=1) - 1
    slot_iota = jnp.arange(cap_panel, dtype=jnp.int32)
    in_slot = (panel_rank[:, None, :] == slot_iota[None, :, None]) & in_panel[:, None, :]
    slot_ids = (jnp.sum(jnp.where(in_slot, by_helper[:, None, :] + 1, 0), axis=2) - 1).reshape(-1)
    own_slot = lax.dynamic_index_in_dim(in_slot, my_helper, 0, keepdims=False)
    picked = product(own_slot.astype(jnp.float32), front_rows)
    head = lax.all_gather(picked[:, :PANEL], "helper", axis=0, tiled=True)
    tail = lax.all_gather(picked[:, PANEL:], "helper", axis=0, tiled=True)
    order = (slot_ids[None, :] == jnp.arange(PANEL, dtype=jnp.int32)[:, None]).astype(jnp.float32)

    own_map = jnp.take(child_map, my_front, axis=0)
    own_cb = own_ids >= PIVOTS
    own_target = jnp.take(own_map, jnp.clip(own_ids - PIVOTS, 0, cb_width - 1))
    device_iota = jnp.arange(devices_all, dtype=jnp.int32)
    owner = jnp.where(own_cb, own_target // parent_rows, devices_all)
    dest_match = owner[:, None] == device_iota[None, :]
    dest_rank = jnp.sum(
        jnp.where(dest_match, jnp.cumsum(dest_match.astype(jnp.int32), axis=0) - 1, 0), axis=1
    )
    send_slot = jnp.where(own_cb, owner * cap_rows + dest_rank, -1)
    send_iota = jnp.arange(devices_all * cap_rows, dtype=jnp.int32)
    pack = send_slot[None, :] == send_iota[:, None]
    send_target = jnp.sum(jnp.where(pack, own_target[None, :] % parent_rows + 1, 0), axis=1) - 1
    targets = lax.all_to_all(
        send_target.astype(jnp.float32).reshape(devices_all, cap_rows),
        ("front", "helper"), split_axis=0, concat_axis=0, tiled=True,
    ).reshape(fronts, 1, helpers * cap_rows)
    pack = pack.astype(jnp.float32)

    inverse = block_inverse(product(order, head))
    active = (own_ids >= PANEL)[:, None]
    current = front_rows[:, :PANEL]
    lower_part = jnp.where(active, product(current, inverse), 0.0)
    lower_slots = product(lower_part, order)

    width = cb_width // CHUNKS
    pieces = [jnp.where(active, lower_part, current)]
    assembled = parent
    arrived = []
    for chunk in range(CHUNKS):
        lo = chunk * width
        block = front_rows[:, PANEL + lo : PANEL + lo + width] - product(
            lower_slots, tail[:, lo : lo + width], lax.Precision.HIGH
        )
        pieces.append(block)
        outgoing = product(pack, block, lax.Precision.HIGH)
        arrived.append(lax.all_to_all(
            outgoing.reshape(devices_all, cap_rows, width),
            ("front", "helper"), split_axis=0, concat_axis=0, tiled=True,
        ))
    for chunk in range(CHUNKS):
        lo = chunk * width
        received = arrived[chunk].reshape(fronts, helpers * cap_rows, width)
        assembled = spread_add(child_map[:, lo : lo + width], targets, received, assembled)
    return (jnp.concatenate(pieces, axis=1)[None], assembled)


def solution(mesh):
    in_specs = (P("front", "helper", None), P(), P(), P(("front", "helper"), None))
    out_specs = (P("front", "helper", None), P(("front", "helper"), None))
    return jax.shard_map(local, mesh=mesh, in_specs=in_specs, out_specs=out_specs, check_vma=False)
```

```python
import jax
import jax.numpy as jnp
from jax import lax
from jax.experimental import pallas as pl
from jax.experimental.pallas import tpu as pltpu
from jax.sharding import PartitionSpec as P

PANEL = 256
PIVOTS = 256
LANES = 128
BLOCK = 32
TILE = 256
WINDOW = 6


def product(left, right, precision=lax.Precision.HIGHEST):
    return jnp.dot(left, right, precision=precision, preferred_element_type=jnp.float32)


def inverse_kernel(matrix_ref, out_ref):
    extent = matrix_ref.shape[0]
    out_ref[...] = matrix_ref[...]
    row_iota = lax.broadcasted_iota(jnp.int32, (BLOCK, 1), 0)
    lane_iota = lax.broadcasted_iota(jnp.int32, (1, extent), 1)
    for start in range(0, extent, BLOCK):
        rows = out_ref[start : start + BLOCK, :]
        for step in range(BLOCK):
            lane = start + step
            column = rows[:, lane : lane + 1]
            pivot_row = rows[step : step + 1, :]
            scale = 1.0 / column[step : step + 1, :]
            at_lane = lane_iota == lane
            scaled = jnp.where(at_lane, scale, pivot_row * scale)
            weight = jnp.where(row_iota == step, -1.0, column)
            keep = jnp.where(at_lane | (row_iota == step), 0.0, rows)
            rows = keep - weight * scaled
        out_ref[start : start + BLOCK, :] = rows
        tile = start // LANES * LANES
        tile_lane = tile + lax.broadcasted_iota(jnp.int32, (1, LANES), 1)
        all_row = lax.broadcasted_iota(jnp.int32, (extent, 1), 0)
        outside = (all_row < start) | (all_row >= start + BLOCK)
        inside_lane = (tile_lane >= start) & (tile_lane < start + BLOCK)
        left = jnp.where(outside & inside_lane, out_ref[:, tile : tile + LANES], 0.0)
        update = product(left, out_ref[tile : tile + LANES, :])
        cleared = outside & (lane_iota >= start) & (lane_iota < start + BLOCK)
        out_ref[...] = jnp.where(cleared, 0.0, out_ref[...]) - update


def block_inverse(matrix):
    extent = matrix.shape[0]
    return pl.pallas_call(
        inverse_kernel,
        out_shape=jax.ShapeDtypeStruct((extent, extent), jnp.float32),
        in_specs=[pl.BlockSpec(memory_space=pltpu.VMEM)],
        out_specs=pl.BlockSpec(memory_space=pltpu.VMEM),
        compiler_params=pltpu.CompilerParams(vmem_limit_bytes=16 * 1024 * 1024),
        cost_estimate=pl.CostEstimate(flops=10**9, bytes_accessed=10**8, transcendentals=0),
        name="panel_inverse",
    )(matrix)


def split(value):
    high = value.astype(jnp.bfloat16)
    return high, (value - high.astype(jnp.float32)).astype(jnp.bfloat16)


def dot(left, right):
    return jnp.dot(left, right, preferred_element_type=jnp.float32)


def outer_update(low_high, low_low, tail):
    tail_high, tail_low = split(tail)
    return dot(low_high, tail_high) + dot(low_high, tail_low) + dot(low_low, tail_high)


def send_kernel(pick_ref, lower_ref, front_ref, tail_ref, *refs):
    out_refs, high_ref, low_ref = refs[:-2], refs[-2], refs[-1]

    @pl.when(pl.program_id(0) == 0)
    def _():
        high_ref[...], low_ref[...] = split(lower_ref[...])

    front_high, front_low = split(front_ref[...])
    pick = pick_ref[...]
    block = dot(pick, front_high) + dot(pick, front_low)
    block = block - outer_update(high_ref[...], low_ref[...], tail_ref[...])
    rows = out_refs[0].shape[0]
    for index, out_ref in enumerate(out_refs):
        out_ref[...] = block[index * rows : (index + 1) * rows]


def send_rows(pick, lower, front_rows, tail, devices_all):
    slots, row_count = pick.shape
    panel_slots, width = tail.shape
    rows = slots // devices_all
    skip = (front_rows.shape[1] - width) // TILE
    fixed = lambda shape: pl.BlockSpec(shape, lambda tile: (0, 0))
    return pl.pallas_call(
        send_kernel,
        grid=(width // TILE,),
        out_shape=[jax.ShapeDtypeStruct((rows, width), jnp.float32)] * devices_all,
        in_specs=[
            fixed(pick.shape),
            fixed(lower.shape),
            pl.BlockSpec((row_count, TILE), lambda tile: (0, tile + skip)),
            pl.BlockSpec((panel_slots, TILE), lambda tile: (0, tile)),
        ],
        out_specs=[pl.BlockSpec((rows, TILE), lambda tile: (0, tile))] * devices_all,
        scratch_shapes=[pltpu.VMEM(lower.shape, jnp.bfloat16)] * 2,
        compiler_params=pltpu.CompilerParams(vmem_limit_bytes=60 * 1024 * 1024),
        cost_estimate=pl.CostEstimate(flops=10**10, bytes_accessed=3 * 10**7, transcendentals=0),
        name="send_rows",
    )(pick, lower, front_rows, tail)


def factor_kernel(left_ref, lower_ref, front_ref, tail_ref, out_ref, high_ref, low_ref):
    tile = pl.program_id(0)

    @pl.when(tile == 0)
    def _():
        out_ref[...] = left_ref[...]
        high_ref[...], low_ref[...] = split(lower_ref[...])

    @pl.when(tile > 0)
    def _():
        out_ref[...] = front_ref[...] - outer_update(high_ref[...], low_ref[...], tail_ref[...])


def factor_rows(left, lower, front_rows, tail):
    row_count, order = front_rows.shape
    panel_slots = tail.shape[0]
    fixed = lambda shape: pl.BlockSpec(shape, lambda tile: (0, 0))
    return pl.pallas_call(
        factor_kernel,
        grid=(order // TILE,),
        out_shape=jax.ShapeDtypeStruct(front_rows.shape, jnp.float32),
        in_specs=[
            fixed(left.shape),
            fixed(lower.shape),
            pl.BlockSpec((row_count, TILE), lambda tile: (0, tile)),
            pl.BlockSpec((panel_slots, TILE), lambda tile: (0, jnp.maximum(tile - 1, 0))),
        ],
        out_specs=pl.BlockSpec((row_count, TILE), lambda tile: (0, tile)),
        scratch_shapes=[pltpu.VMEM(lower.shape, jnp.bfloat16)] * 2,
        compiler_params=pltpu.CompilerParams(vmem_limit_bytes=60 * 1024 * 1024),
        cost_estimate=pl.CostEstimate(flops=10**10, bytes_accessed=3 * 10**7, transcendentals=0),
        name="factor_rows",
    )(left, lower, front_rows, tail)


def spread_kernel(map_ref, target_ref, base_ref, *refs):
    received_refs, out_ref, turned, spread = refs[:-3], refs[-3], refs[-2], refs[-1]
    index = pl.program_id(0)
    width, slots = turned.shape
    parent_rows, piece = out_ref.shape

    @pl.when(index == 0)
    def _():
        spread[...] = jnp.zeros_like(spread)
        for first in range(0, width, LANES):
            parts = [ref[:, first : first + LANES] for ref in received_refs]
            block = jnp.concatenate(parts, axis=0) if len(parts) > 1 else parts[0]
            turned[first : first + LANES, :] = block.T

        @pl.loop(0, width // 16)
        def _(group):
            base = group * 16
            for offset in range(16):
                place = map_ref[base + offset]
                spread[pl.ds(place, 1), :] = turned[pl.ds(base + offset, 1), :]

    row_iota = lax.broadcasted_iota(jnp.int32, (parent_rows, slots), 0)
    pick = (row_iota == target_ref[...].astype(jnp.int32)).astype(jnp.bfloat16)
    pick = jnp.concatenate([pick, pick], axis=1)
    at = pl.ds(pl.multiple_of(index * piece, piece), piece)
    both = jnp.concatenate(split(spread[at, :]), axis=1)
    out_ref[...] = base_ref[...] + lax.dot_general(
        pick, both, (((1,), (1,)), ((), ())), preferred_element_type=jnp.float32
    )


def spread_add(columns, targets, received, base):
    width = columns.shape[0]
    slots = targets.shape[1]
    parent_rows, parent_width = base.shape
    piece = 1024
    block = pl.BlockSpec((parent_rows, piece), lambda index: (0, index))
    whole = lambda array: pl.BlockSpec(array.shape, lambda index: (0, 0))
    return pl.pallas_call(
        spread_kernel,
        grid=(parent_width // piece,),
        out_shape=jax.ShapeDtypeStruct(base.shape, jnp.float32),
        in_specs=[pl.BlockSpec(memory_space=pltpu.SMEM), whole(targets), block]
        + [whole(array) for array in received],
        out_specs=block,
        scratch_shapes=[
            pltpu.VMEM((width, slots), jnp.float32),
            pltpu.VMEM((parent_width, slots), jnp.float32),
        ],
        compiler_params=pltpu.CompilerParams(vmem_limit_bytes=60 * 1024 * 1024),
        cost_estimate=pl.CostEstimate(flops=10**10, bytes_accessed=5 * 10**7, transcendentals=0),
        name="spread_add",
    )(columns, targets, base, *received)


def local(front, row_list, child_map, parent):
    front_rows = front[0]
    row_count = front_rows.shape[0]
    helpers = lax.axis_size("helper")
    fronts = lax.axis_size("front")
    devices_all = helpers * fronts
    my_front = lax.axis_index("front")
    my_helper = lax.axis_index("helper")
    parent_rows = parent.shape[0]
    cb_width = front_rows.shape[1] - PIVOTS
    cap_rows = (row_count + devices_all - 1) // devices_all
    cap_panel = 3 * PANEL // (2 * helpers)
    front_order = jnp.take(row_list, my_front, axis=0)
    own_ids = lax.dynamic_slice_in_dim(front_order, my_helper * row_count, row_count)

    by_helper = front_order.reshape(helpers, row_count)
    in_panel = by_helper < PANEL
    panel_rank = jnp.cumsum(in_panel.astype(jnp.int32), axis=1) - 1
    slot_iota = jnp.arange(cap_panel, dtype=jnp.int32)
    in_slot = (panel_rank[:, None, :] == slot_iota[None, :, None]) & in_panel[:, None, :]
    slot_ids = (jnp.sum(jnp.where(in_slot, by_helper[:, None, :] + 1, 0), axis=2) - 1).reshape(-1)
    own_slot = lax.dynamic_index_in_dim(in_slot, my_helper, 0, keepdims=False)
    own_slot = own_slot.astype(jnp.float32)
    head = lax.all_gather(product(own_slot, front_rows[:, :PANEL]), "helper", axis=0, tiled=True)
    tail = lax.all_gather(product(own_slot, front_rows[:, PANEL:]), "helper", axis=0, tiled=True)
    order = (slot_ids[None, :] == jnp.arange(PANEL, dtype=jnp.int32)[:, None]).astype(jnp.float32)

    own_map = jnp.take(child_map, my_front, axis=0)
    own_cb = own_ids >= PIVOTS
    own_target = jnp.take(own_map, jnp.clip(own_ids - PIVOTS, 0, cb_width - 1))
    device_iota = jnp.arange(devices_all, dtype=jnp.int32)
    owner = jnp.where(own_cb, own_target // parent_rows, devices_all)
    dest_match = owner[:, None] == device_iota[None, :]
    dest_rank = jnp.sum(
        jnp.where(dest_match, jnp.cumsum(dest_match.astype(jnp.int32), axis=0) - 1, 0), axis=1
    )
    me_flat = my_front * helpers + my_helper
    send_slot = jnp.where(own_cb, (owner ^ me_flat) * cap_rows + dest_rank, -1)
    send_iota = jnp.arange(devices_all * cap_rows, dtype=jnp.int32)
    pack = send_slot[None, :] == send_iota[:, None]
    send_target = jnp.sum(jnp.where(pack, own_target[None, :] % parent_rows + 1, 0), axis=1) - 1
    targets = lax.all_to_all(
        jnp.take(send_target.astype(jnp.float32).reshape(devices_all, cap_rows), device_iota ^ me_flat, axis=0),
        ("front", "helper"), split_axis=0, concat_axis=0, tiled=True,
    )
    targets = jnp.take(targets, device_iota ^ me_flat, axis=0).reshape(fronts, 1, helpers * cap_rows)

    inverse = block_inverse(product(order, head))
    active = (own_ids >= PANEL)[:, None]
    current = front_rows[:, :PANEL]
    lower_part = jnp.where(active, product(current, inverse), 0.0)
    lower_slots = product(lower_part, order)

    pack_lower = product(pack.astype(jnp.float32), lower_slots)
    outgoing = send_rows(pack.astype(jnp.bfloat16), pack_lower, front_rows, tail, devices_all)
    near = [offset for offset in range(1, devices_all // 2)]
    far = [offset for offset in range(devices_all // 2, devices_all)]
    sequence = []
    while near or far:
        sequence += far[:1] + near[:2]
        far, near = far[1:], near[2:]
    arrived = list(outgoing)
    for index, offset in enumerate(sequence):
        pairs = [(device, device ^ offset) for device in range(devices_all)]
        piece = outgoing[offset]
        if index >= WINDOW:
            before = sequence[index - WINDOW]
            piece, arrived[before] = lax.optimization_barrier((piece, arrived[before]))
        arrived[offset] = lax.ppermute(piece, ("front", "helper"), pairs)
    factors = factor_rows(jnp.where(active, lower_part, current), lower_slots, front_rows, tail)
    assembled = parent
    for front_offset in range(fronts):
        columns = jnp.take(child_map, my_front ^ front_offset, axis=0)
        received = arrived[front_offset * helpers : (front_offset + 1) * helpers]
        if cap_rows % 8:
            received = [jnp.concatenate(received, axis=0)]
        assembled = spread_add(columns, targets[front_offset], received, assembled)
    return (factors[None], assembled)


def solution(mesh):
    in_specs = (P("front", "helper", None), P(), P(), P(("front", "helper"), None))
    out_specs = (P("front", "helper", None), P(("front", "helper"), None))
    return jax.shard_map(local, mesh=mesh, in_specs=in_specs, out_specs=out_specs, check_vma=False)
```

```python
import jax
import jax.numpy as jnp
from jax import lax
from jax.experimental import pallas as pl
from jax.experimental.pallas import tpu as pltpu
from jax.sharding import PartitionSpec as P

PANEL = 256
PIVOTS = 256
LANES = 128
BLOCK = 32
TILE = 256
WINDOW = 6


def product(left, right, precision=lax.Precision.HIGHEST):
    return jnp.dot(left, right, precision=precision, preferred_element_type=jnp.float32)


def inverse_kernel(matrix_ref, out_ref):
    extent = matrix_ref.shape[0]
    out_ref[...] = matrix_ref[...]
    row_iota = lax.broadcasted_iota(jnp.int32, (BLOCK, 1), 0)
    lane_iota = lax.broadcasted_iota(jnp.int32, (1, extent), 1)
    for start in range(0, extent, BLOCK):
        rows = out_ref[start : start + BLOCK, :]
        for step in range(BLOCK):
            lane = start + step
            column = rows[:, lane : lane + 1]
            pivot_row = rows[step : step + 1, :]
            scale = 1.0 / column[step : step + 1, :]
            at_lane = lane_iota == lane
            scaled = jnp.where(at_lane, scale, pivot_row * scale)
            weight = jnp.where(row_iota == step, -1.0, column)
            keep = jnp.where(at_lane | (row_iota == step), 0.0, rows)
            rows = keep - weight * scaled
        out_ref[start : start + BLOCK, :] = rows
        tile = start // LANES * LANES
        tile_lane = tile + lax.broadcasted_iota(jnp.int32, (1, LANES), 1)
        all_row = lax.broadcasted_iota(jnp.int32, (extent, 1), 0)
        outside = (all_row < start) | (all_row >= start + BLOCK)
        inside_lane = (tile_lane >= start) & (tile_lane < start + BLOCK)
        left = jnp.where(outside & inside_lane, out_ref[:, tile : tile + LANES], 0.0)
        update = product(left, out_ref[tile : tile + LANES, :])
        cleared = outside & (lane_iota >= start) & (lane_iota < start + BLOCK)
        out_ref[...] = jnp.where(cleared, 0.0, out_ref[...]) - update


def block_inverse(matrix):
    extent = matrix.shape[0]
    return pl.pallas_call(
        inverse_kernel,
        out_shape=jax.ShapeDtypeStruct((extent, extent), jnp.float32),
        in_specs=[pl.BlockSpec(memory_space=pltpu.VMEM)],
        out_specs=pl.BlockSpec(memory_space=pltpu.VMEM),
        compiler_params=pltpu.CompilerParams(vmem_limit_bytes=16 * 1024 * 1024),
        cost_estimate=pl.CostEstimate(flops=10**9, bytes_accessed=10**8, transcendentals=0),
        name="panel_inverse",
    )(matrix)


def split(value):
    high = value.astype(jnp.bfloat16)
    return high, (value - high.astype(jnp.float32)).astype(jnp.bfloat16)


def dot(left, right):
    return jnp.dot(left, right, preferred_element_type=jnp.float32)


def outer_update(low_high, low_low, tail):
    tail_high, tail_low = split(tail)
    return dot(low_high, tail_high) + dot(low_high, tail_low) + dot(low_low, tail_high)


def send_kernel(pick_ref, lower_ref, front_ref, tail_ref, *refs):
    out_refs, high_ref, low_ref = refs[:-2], refs[-2], refs[-1]

    @pl.when(pl.program_id(0) == 0)
    def _():
        high_ref[...], low_ref[...] = split(lower_ref[...])

    front_high, front_low = split(front_ref[...])
    pick = pick_ref[...]
    block = dot(pick, front_high) + dot(pick, front_low)
    block = block - outer_update(high_ref[...], low_ref[...], tail_ref[...])
    rows = out_refs[0].shape[0]
    for index, out_ref in enumerate(out_refs):
        out_ref[...] = block[index * rows : (index + 1) * rows]


def send_rows(pick, lower, front_rows, tail, devices_all):
    slots, row_count = pick.shape
    panel_slots, width = tail.shape
    rows = slots // devices_all
    skip = (front_rows.shape[1] - width) // TILE
    fixed = lambda shape: pl.BlockSpec(shape, lambda tile: (0, 0))
    return pl.pallas_call(
        send_kernel,
        grid=(width // TILE,),
        out_shape=[jax.ShapeDtypeStruct((rows, width), jnp.float32)] * devices_all,
        in_specs=[
            fixed(pick.shape),
            fixed(lower.shape),
            pl.BlockSpec((row_count, TILE), lambda tile: (0, tile + skip)),
            pl.BlockSpec((panel_slots, TILE), lambda tile: (0, tile)),
        ],
        out_specs=[pl.BlockSpec((rows, TILE), lambda tile: (0, tile))] * devices_all,
        scratch_shapes=[pltpu.VMEM(lower.shape, jnp.bfloat16)] * 2,
        compiler_params=pltpu.CompilerParams(vmem_limit_bytes=60 * 1024 * 1024),
        cost_estimate=pl.CostEstimate(flops=10**10, bytes_accessed=3 * 10**7, transcendentals=0),
        name="send_rows",
    )(pick, lower, front_rows, tail)


def factor_kernel(left_ref, lower_ref, front_ref, tail_ref, out_ref, high_ref, low_ref):
    tile = pl.program_id(0)

    @pl.when(tile == 0)
    def _():
        out_ref[...] = left_ref[...]
        high_ref[...], low_ref[...] = split(lower_ref[...])

    @pl.when(tile > 0)
    def _():
        out_ref[...] = front_ref[...] - outer_update(high_ref[...], low_ref[...], tail_ref[...])


def factor_rows(left, lower, front_rows, tail):
    row_count, order = front_rows.shape
    panel_slots = tail.shape[0]
    fixed = lambda shape: pl.BlockSpec(shape, lambda tile: (0, 0))
    return pl.pallas_call(
        factor_kernel,
        grid=(order // TILE,),
        out_shape=jax.ShapeDtypeStruct(front_rows.shape, jnp.float32),
        in_specs=[
            fixed(left.shape),
            fixed(lower.shape),
            pl.BlockSpec((row_count, TILE), lambda tile: (0, tile)),
            pl.BlockSpec((panel_slots, TILE), lambda tile: (0, jnp.maximum(tile - 1, 0))),
        ],
        out_specs=pl.BlockSpec((row_count, TILE), lambda tile: (0, tile)),
        scratch_shapes=[pltpu.VMEM(lower.shape, jnp.bfloat16)] * 2,
        compiler_params=pltpu.CompilerParams(vmem_limit_bytes=60 * 1024 * 1024),
        cost_estimate=pl.CostEstimate(flops=10**10, bytes_accessed=3 * 10**7, transcendentals=0),
        name="factor_rows",
    )(left, lower, front_rows, tail)


def spread_kernel(map_ref, target_ref, base_ref, *refs):
    received_refs, out_ref, turned, spread = refs[:-3], refs[-3], refs[-2], refs[-1]
    index = pl.program_id(0)
    width, slots = turned.shape
    parent_rows, piece = out_ref.shape

    @pl.when(index == 0)
    def _():
        spread[...] = jnp.zeros_like(spread)
        for first in range(0, width, LANES):
            parts = [ref[:, first : first + LANES] for ref in received_refs]
            block = jnp.concatenate(parts, axis=0) if len(parts) > 1 else parts[0]
            turned[first : first + LANES, :] = block.T

        @pl.loop(0, width // 16)
        def _(group):
            base = group * 16
            for offset in range(16):
                place = map_ref[base + offset]
                spread[pl.ds(place, 1), :] = turned[pl.ds(base + offset, 1), :]

    row_iota = lax.broadcasted_iota(jnp.int32, (parent_rows, slots), 0)
    pick = (row_iota == target_ref[...].astype(jnp.int32)).astype(jnp.bfloat16)
    pick = jnp.concatenate([pick, pick], axis=1)
    at = pl.ds(pl.multiple_of(index * piece, piece), piece)
    both = jnp.concatenate(split(spread[at, :]), axis=1)
    out_ref[...] = base_ref[...] + lax.dot_general(
        pick, both, (((1,), (1,)), ((), ())), preferred_element_type=jnp.float32
    )


def spread_add(columns, targets, received, base):
    width = columns.shape[0]
    slots = targets.shape[1]
    parent_rows, parent_width = base.shape
    piece = 1024
    block = pl.BlockSpec((parent_rows, piece), lambda index: (0, index))
    whole = lambda array: pl.BlockSpec(array.shape, lambda index: (0, 0))
    return pl.pallas_call(
        spread_kernel,
        grid=(parent_width // piece,),
        out_shape=jax.ShapeDtypeStruct(base.shape, jnp.float32),
        in_specs=[pl.BlockSpec(memory_space=pltpu.SMEM), whole(targets), block]
        + [whole(array) for array in received],
        out_specs=block,
        scratch_shapes=[
            pltpu.VMEM((width, slots), jnp.float32),
            pltpu.VMEM((parent_width, slots), jnp.float32),
        ],
        compiler_params=pltpu.CompilerParams(vmem_limit_bytes=60 * 1024 * 1024),
        cost_estimate=pl.CostEstimate(flops=10**10, bytes_accessed=5 * 10**7, transcendentals=0),
        name="spread_add",
    )(columns, targets, base, *received)


def local(front, row_list, child_map, parent):
    front_rows = front[0]
    row_count = front_rows.shape[0]
    helpers = lax.axis_size("helper")
    fronts = lax.axis_size("front")
    devices_all = helpers * fronts
    my_front = lax.axis_index("front")
    my_helper = lax.axis_index("helper")
    parent_rows = parent.shape[0]
    cb_width = front_rows.shape[1] - PIVOTS
    cap_rows = (row_count + devices_all - 1) // devices_all
    cap_panel = 3 * PANEL // (2 * helpers)
    front_order = jnp.take(row_list, my_front, axis=0)
    own_ids = lax.dynamic_slice_in_dim(front_order, my_helper * row_count, row_count)

    by_helper = front_order.reshape(helpers, row_count)
    in_panel = by_helper < PANEL
    panel_rank = jnp.cumsum(in_panel.astype(jnp.int32), axis=1) - 1
    slot_iota = jnp.arange(cap_panel, dtype=jnp.int32)
    in_slot = (panel_rank[:, None, :] == slot_iota[None, :, None]) & in_panel[:, None, :]
    slot_ids = (jnp.sum(jnp.where(in_slot, by_helper[:, None, :] + 1, 0), axis=2) - 1).reshape(-1)
    own_slot = lax.dynamic_index_in_dim(in_slot, my_helper, 0, keepdims=False)
    own_slot = own_slot.astype(jnp.float32)
    head = lax.all_gather(product(own_slot, front_rows[:, :PANEL]), "helper", axis=0, tiled=True)
    tail = lax.all_gather(product(own_slot, front_rows[:, PANEL:]), "helper", axis=0, tiled=True)
    order = (slot_ids[None, :] == jnp.arange(PANEL, dtype=jnp.int32)[:, None]).astype(jnp.float32)

    own_map = jnp.take(child_map, my_front, axis=0)
    own_cb = own_ids >= PIVOTS
    own_target = jnp.take(own_map, jnp.clip(own_ids - PIVOTS, 0, cb_width - 1))
    device_iota = jnp.arange(devices_all, dtype=jnp.int32)
    owner = jnp.where(own_cb, own_target // parent_rows, devices_all)
    dest_match = owner[:, None] == device_iota[None, :]
    dest_rank = jnp.sum(
        jnp.where(dest_match, jnp.cumsum(dest_match.astype(jnp.int32), axis=0) - 1, 0), axis=1
    )
    me_flat = my_front * helpers + my_helper
    send_slot = jnp.where(own_cb, (owner ^ me_flat) * cap_rows + dest_rank, -1)
    send_iota = jnp.arange(devices_all * cap_rows, dtype=jnp.int32)
    pack = send_slot[None, :] == send_iota[:, None]
    send_target = jnp.sum(jnp.where(pack, own_target[None, :] % parent_rows + 1, 0), axis=1) - 1
    targets = lax.all_to_all(
        jnp.take(send_target.astype(jnp.float32).reshape(devices_all, cap_rows), device_iota ^ me_flat, axis=0),
        ("front", "helper"), split_axis=0, concat_axis=0, tiled=True,
    )
    targets = jnp.take(targets, device_iota ^ me_flat, axis=0).reshape(fronts, 1, helpers * cap_rows)

    matrix, targets = lax.optimization_barrier((product(order, head), targets))
    inverse = block_inverse(matrix)
    active = (own_ids >= PANEL)[:, None]
    current = front_rows[:, :PANEL]
    lower_part = jnp.where(active, product(current, inverse), 0.0)
    lower_slots = product(lower_part, order)

    pack_lower = product(pack.astype(jnp.float32), lower_slots)
    outgoing = send_rows(pack.astype(jnp.bfloat16), pack_lower, front_rows, tail, devices_all)
    near = [offset for offset in range(1, devices_all // 2)]
    far = [offset for offset in range(devices_all // 2, devices_all)]
    sequence = []
    while near or far:
        sequence += far[:1] + near[:1] + far[1:2] + near[1:3]
        far, near = far[2:], near[3:]
    arrived = list(outgoing)
    for index, offset in enumerate(sequence):
        pairs = [(device, device ^ offset) for device in range(devices_all)]
        piece = outgoing[offset]
        if index >= WINDOW:
            before = sequence[index - WINDOW]
            piece, arrived[before] = lax.optimization_barrier((piece, arrived[before]))
        arrived[offset] = lax.ppermute(piece, ("front", "helper"), pairs)
    factors = factor_rows(jnp.where(active, lower_part, current), lower_slots, front_rows, tail)
    assembled = parent
    for front_offset in range(fronts):
        columns = jnp.take(child_map, my_front ^ front_offset, axis=0)
        received = arrived[front_offset * helpers : (front_offset + 1) * helpers]
        if cap_rows % 8:
            received = [jnp.concatenate(received, axis=0)]
        assembled = spread_add(columns, targets[front_offset], received, assembled)
    return (factors[None], assembled)


def solution(mesh):
    in_specs = (P("front", "helper", None), P(), P(), P(("front", "helper"), None))
    out_specs = (P("front", "helper", None), P(("front", "helper"), None))
    return jax.shard_map(local, mesh=mesh, in_specs=in_specs, out_specs=out_specs, check_vma=False)
```
